512 devices in a mesh: st: 64 (over z_lo, y, core), hd: 8 (over x, z_hi).
Axes of the slice: x: 4, y: 4, z: 16 (z_hi: 2, z_lo: 8; z = z_hi * 8 + z_lo), core: 2. Of those that a mesh axis runs over, the one named last changes fastest.
Arguments:
- queries: bfloat16 [8192, 3072], P('st', 'hd'), may hold values from -160 to 160
- keys: bfloat16 [8192, 3072], P('st', 'hd'), may hold values from -6 to 6
- values: bfloat16 [8192, 3072], P('st', 'hd'), may hold values from -6 to 6
- grad_out: bfloat16 [8192, 3072], P('st', 'hd'), may hold values from -6 to 6
- head_window: int32 [24, 3], P('hd'), may hold values from 0 to 1, as said below
Outputs:
- attended: bfloat16 [8192, 3072], P('st', 'hd')
- grad_queries: bfloat16 [8192, 3072], P('st', 'hd')
- grad_keys: bfloat16 [8192, 3072], P('st', 'hd')
- grad_values: bfloat16 [8192, 3072], P('st', 'hd')
The draws below stay inside these ranges and needn't reach their ends.
Inputs may be any that keep to these rules, and one draw needn't show every extreme that they name: `head_window`: some head has radius 1 in all three directions and some head radius 0 in all three.
All inputs are finite; a program needn't handle non-finite values.
Results may differ from the reference program's by a relative error of at most 0.013.
Values may be sent and summed in bfloat16 or wider, within the bound.
A program may use at most 64 MiB of HBM per device.

```python
import jax
import jax.numpy as jnp
import numpy as np
from jax import lax

HEADS = 24
HD = 128
GH = 4
GW = 4
TILE = 128
TOKENS = 8192
N_ST = 64


def shared_rows(key):
    base = jnp.clip(jax.random.normal(key, (TOKENS, HEADS * HD), jnp.float32), -6.0, 6.0)
    return base


def draw_keys(key, part):
    base = shared_rows(key)
    return base.astype(jnp.bfloat16)


def draw_queries(key, part):
    key = jax.random.fold_in(key, 2)
    fresh = jnp.clip(jax.random.normal(key, (TOKENS, HEADS * HD), jnp.float32), -6.0, 6.0)
    return fresh.astype(jnp.bfloat16)


def draw_head_window(key, part):
    key = jax.random.fold_in(key, 3)
    radius = jax.random.randint(key, (HEADS, 3), 0, 2)
    order = jax.random.permutation(jax.random.fold_in(key, 7), HEADS)
    heads = jnp.arange(HEADS)
    radius = jnp.where((heads == order[0])[:, None], 1, radius)
    radius = jnp.where((heads == order[1])[:, None], 0, radius)
    return radius.astype(jnp.int32)


def block_scale(own_key, dims, pieces, least, top_value):
    def one(position, shards_of):
        heights = jax.random.uniform(jax.random.fold_in(jax.random.fold_in(own_key, 6), position), (shards_of,), jnp.float32, least / len(pieces), top_value / len(pieces))
        return jnp.repeat(jnp.exp(heights), dims[position] // shards_of).reshape((-1,) + (1,) * (len(dims) - position - 1))

    factor_of = one(*pieces[0])
    for cut in pieces[1:]:
        factor_of = factor_of * one(*cut)
    return factor_of


def normal_values(stream_key, shape, scale, bound, cuts=(), kind=jnp.bfloat16):
    gain = block_scale(stream_key, shape, cuts, -0.22, 0.18) if cuts else 1.0
    entries = jax.random.normal(stream_key, shape, jnp.float32) * scale * gain
    return jnp.minimum(jnp.maximum(entries, -bound), bound).astype(kind)


def setup_inputs(seed: int = 0) -> dict:
    splits = jax.random.split(jax.random.key(seed), 6)
    return {
        "queries": draw_queries(jax.random.fold_in(splits[5], 71), 0),
        "keys": draw_keys(jax.random.fold_in(splits[5], 71), 0),
        "values": normal_values(splits[2], (TOKENS, HEADS * HD), 1.0, 6.0, ((0, 64), (1, 8))),
        "grad_out": normal_values(splits[3], (TOKENS, HEADS * HD), 1.0, 6.0, ((0, 64), (1, 8))),
        "head_window": draw_head_window(jax.random.fold_in(splits[5], 71), 0),
    }


OFFSETS = np.array([[a, b, c] for a in (-1, 0, 1) for b in (-1, 0, 1) for c in (-1, 0, 1)], dtype=np.int32)


def reference(queries, keys, values, grad_out, head_window):
    grid_t = N_ST // (GH * GW)
    scale = HD ** -0.5
    shape4 = (N_ST, TILE, HEADS, HD)
    q_all = queries.reshape(shape4)
    k_all = keys.reshape(shape4)
    v_all = values.reshape(shape4)
    g_all = grad_out.reshape(shape4)
    steps = jnp.asarray(OFFSETS)
    headmask = jnp.all(jnp.abs(steps)[None, :, :] <= head_window[:, None, :], axis=2)
    limits = jnp.array([grid_t, GH, GW], jnp.int32)

    def per_tile(carry, place):
        acc_keys, acc_values = carry
        pos = jnp.stack([place // (GH * GW), (place // GW) % GH, place % GW]).astype(jnp.int32)
        target = pos[None, :] + steps
        valid = jnp.all((target >= 0) & (target < limits[None, :]), axis=1)
        nidx = jnp.where(valid, (target[:, 0] * GH + target[:, 1]) * GW + target[:, 2], 0).astype(jnp.int32)
        qt = q_all[place].astype(jnp.float32)
        gt = g_all[place].astype(jnp.float32)
        kk = k_all[nidx].astype(jnp.float32)
        vv = v_all[nidx].astype(jnp.float32)
        scores = jnp.einsum('ihd,njhd->hinj', qt, kk) * scale
        mask = headmask[:, None, :, None] & valid[None, None, :, None]
        scores = jnp.where(mask, scores, -jnp.inf)
        top = jnp.max(scores, axis=(2, 3), keepdims=True)
        expd = jnp.exp(scores - top)
        probs = expd / jnp.sum(expd, axis=(2, 3), keepdims=True)
        probs_low = probs.astype(jnp.bfloat16).astype(jnp.float32)
        out_full = jnp.einsum('hinj,njhd->ihd', probs_low, vv)
        dprobs = jnp.einsum('ihd,njhd->hinj', gt, vv)
        delta = jnp.sum(gt * out_full, axis=2)
        dscores = (probs * (dprobs - jnp.transpose(delta)[:, :, None, None])).astype(jnp.bfloat16).astype(jnp.float32)
        grad_q = (jnp.einsum('hinj,njhd->ihd', dscores, kk) * scale).astype(jnp.bfloat16)
        part_k = (jnp.einsum('hinj,ihd->njhd', dscores, qt) * scale).astype(jnp.bfloat16).astype(jnp.float32)
        part_v = jnp.einsum('hinj,ihd->njhd', probs_low, gt).astype(jnp.bfloat16).astype(jnp.float32)
        keep = valid.astype(part_k.dtype)[:, None, None, None]
        acc_keys = acc_keys.at[nidx].add(part_k * keep)
        acc_values = acc_values.at[nidx].add(part_v * keep)
        return (acc_keys, acc_values), (out_full.astype(jnp.bfloat16), grad_q)

    start = (jnp.zeros(shape4, jnp.float32), jnp.zeros(shape4, jnp.float32))
    (acc_keys, acc_values), (attended, grad_queries) = lax.scan(per_tile, start, jnp.arange(N_ST, dtype=jnp.int32))
    flat = (TOKENS, HEADS * HD)
    return (attended.reshape(flat), grad_queries.reshape(flat),
            acc_keys.astype(jnp.bfloat16).reshape(flat), acc_values.astype(jnp.bfloat16).reshape(flat))
```

```python
import functools
import math

import jax
import jax.numpy as jnp
from jax import lax
from jax.experimental import pallas as pl
from jax.experimental.pallas import tpu as pltpu
from jax.sharding import PartitionSpec as P

HD = 128
TILE = 128
FRAMES = 4
HEADS_HERE = 3
SCALE = HD ** (-0.5)
EXP2_SCALE = SCALE * math.log2(math.e)
MESH = pl.DeviceIdType.MESH
BF16 = jnp.bfloat16
F32 = jnp.float32

OWN = ((0, 0), (0, 1), (1, 1), (1, 0))
HERE, OUT, IN = 0, 1, 2
ROWS = 9
K, V, Q, G, STATS = range(5)
Q_ALL = 4 * TILE


def blocks(lh):
    if lh < 2:
        return ((0, 0, 4 * TILE), (1, 0, 4 * TILE), (2, TILE, 2 * TILE))
    return ((0, 2 * TILE, 2 * TILE), (1, 2 * TILE, 2 * TILE), (2, 2 * TILE, TILE))


def pieces(lh):
    if lh < 2:
        return ((0, 2, 0, 4 * TILE), (2, 1, TILE, 2 * TILE))
    return ((0, 2, 2 * TILE, 2 * TILE), (2, 1, 2 * TILE, TILE))


def dot_nt(a, b):
    return lax.dot_general(a, b, (((1,), (1,)), ((), ())), preferred_element_type=F32)


def dot_tn(a, b):
    return lax.dot_general(a, b, (((0,), (0,)), ((), ())), preferred_element_type=F32)


def dot_nn(a, b):
    return lax.dot_general(a, b, (((1,), (0,)), ((), ())), preferred_element_type=F32)


def kernel(
    q_ref, k_ref, v_ref, g_ref, win_hbm,
    out_ref, gq_ref, gk_ref, gv_ref,
    kbuf, vbuf, qbuf, gbuf, stats, k_own, v_own, q_own, g_own, s_buf, dp_buf, p_low, ds_low, top_ref, sum_ref,
    out_t, gq_t, gk_t, gv_t, results, win_ref,
    own_send, own_recv, far_send, far_recv, chain_send, chain_recv, across_send, across_recv,
    fin_send, fin_recv, win_sem,
):
    pltpu.make_async_copy(win_hbm, win_ref, win_sem).start()
    inputs = (k_ref, v_ref, q_ref, g_ref)
    bufs = (kbuf, vbuf, qbuf, gbuf, stats)
    own = (k_own, v_own, q_own, g_own)
    place = lax.axis_index("st")
    t = place // 16
    upper = (place // 8) % 2
    col = (place // 2) % 4
    core = place % 2
    active = col < HEADS_HERE
    row = (place // 4) % 4
    column = place % 4
    w_half = column // 2
    lh_own = (row + upper) % 2
    lw_own = (column + w_half) % 2
    is_self = jnp.logical_and(active, w_half == core)
    outward = 2 * upper - 1
    t_out = t + outward
    t_in = t - outward
    has_out = jnp.logical_and(t_out >= 0, t_out < FRAMES)
    has_in = jnp.logical_and(t_in >= 0, t_in < FRAMES)
    other_core = place + 1 - 2 * core
    mate = place - 8 * outward
    outer = place + 8 * outward
    out2 = place + 16 * outward
    in2 = place - 16 * outward
    in3 = place - 24 * outward

    def worker(head):
        return (2 * t + upper) * 8 + 2 * head + w_half

    def owner(n):
        a, b = OWN[n]
        r = upper * (3 - a) + (1 - upper) * a
        c = core * (3 - b) + (1 - core) * b
        return t * 16 + r * 4 + c

    def far_owner(n, frame):
        a, b = OWN[n]
        r = upper * (3 - a) + (1 - upper) * a
        c = core * (3 - b) + (1 - core) * b
        return frame * 16 + r * 4 + c

    def remote(src, dst, send, recv, device):
        return pltpu.make_async_remote_copy(
            src_ref=src, dst_ref=dst, send_sem=send, recv_sem=recv,
            device_id={"st": device}, device_id_type=MESH,
        )

    def wait_for(dst, sem):
        pltpu.make_async_copy(dst, dst, sem).wait()

    barrier = pltpu.get_barrier_semaphore()

    def greet(device):
        pl.semaphore_signal(barrier, inc=1, device_id={"st": device}, device_id_type=MESH)

    at_edge = lh_own == 0

    def far_worker(side, head):
        return worker(head) + (-16, 16)[side] * outward

    far_flag = (has_in, has_out)
    for head in range(HEADS_HERE):
        @pl.when(worker(head) != place)
        def _():
            greet(worker(head))

        for side in range(2):
            @pl.when(jnp.logical_and(at_edge, far_flag[side]))
            def _():
                greet(far_worker(side, head))

    @pl.when(active)
    def _():
        for n in range(4):
            @pl.when(owner(n) != place)
            def _():
                greet(owner(n))

        greet(other_core)
        greet(mate)

        @pl.when(has_out)
        def _():
            greet(outer)
            greet(out2)
            for n in range(2):
                greet(far_owner(n, t_out))

        @pl.when(has_in)
        def _():
            greet(in2)
            greet(in3)
            for n in range(2):
                greet(far_owner(n, t_in))

    as_int = lambda flag: flag.astype(jnp.int32)
    selfs = as_int(is_self)
    greeted = 3 - selfs + 3 * as_int(at_edge) * (as_int(has_in) + as_int(has_out))
    pl.semaphore_wait(
        barrier, greeted + as_int(active) * (6 - selfs + 4 * as_int(has_out) + 4 * as_int(has_in))
    )

    def head_cols(ref, head):
        return ref.at[:, pl.ds(head * HD, HD)]

    def own_copy(which, head):
        return remote(
            head_cols(inputs[which], head), bufs[which].at[HERE, lh_own, lw_own],
            own_send.at[which], own_recv.at[lh_own, which], worker(head),
        )

    def far_copy(which, side, head):
        return remote(
            head_cols(inputs[which], head), bufs[which].at[(OUT, IN)[side], 0, lw_own],
            far_send.at[side, which], far_recv.at[side, which], far_worker(side, head),
        )

    def send_own(which):
        for head in range(HEADS_HERE):
            mine = worker(head) == place

            @pl.when(mine)
            def _():
                pltpu.make_async_copy(
                    head_cols(inputs[which], head), bufs[which].at[HERE, lh_own, lw_own], own_recv.at[lh_own, which]
                ).start()

            @pl.when(jnp.logical_not(mine))
            def _():
                own_copy(which, head).start()

    def own_left(which):
        ref = inputs[which]

        @pl.when(is_self)
        def _():
            wait_for(ref.at[:, pl.ds(0, (HEADS_HERE - 1) * HD)], own_send.at[which])

        @pl.when(jnp.logical_not(is_self))
        def _():
            wait_for(ref, own_send.at[which])

    def send_far(which):
        for side in range(2):
            @pl.when(jnp.logical_and(at_edge, far_flag[side]))
            def _():
                for head in range(HEADS_HERE):
                    far_copy(which, side, head).start()

    for which in (K, Q, V, G):
        send_own(which)

    @pl.when(jnp.logical_not(active))
    def _():
        for which in (K, Q, V, G):
            own_left(which)
        for which in (K, V, Q, G):
            send_far(which)

    CHAIN = {
        1: ((HERE, 1), (HERE, 2), mate, None, None),
        2: ((HERE, 1), (OUT, 2), outer, has_out, has_out),
        3: ((HERE, 2), (OUT, 1), outer, has_out, has_out),
        4: ((HERE, 0), (OUT, 0), in2, has_in, has_out),
        5: ((HERE, 0), (IN, 0), out2, has_out, has_in),
        6: ((OUT, 2), (IN, 1), mate, has_out, has_in),
        7: ((OUT, 1), (IN, 2), mate, has_out, has_in),
    }
    STATS_TO = {
        1: CHAIN[1],
        2: CHAIN[2],
        3: ((HERE, 1), (OUT, 1), in2, has_in, has_out),
        4: CHAIN[4],
        5: CHAIN[5],
        6: ((HERE, 1), (IN, 1), out2, has_out, has_in),
        7: ((HERE, 1), (IN, 2), in3, has_in, has_in),
    }

    def route(which, number):
        return (STATS_TO if which == STATS else CHAIN)[number]

    def only(flag, run):
        if flag is None:
            run()
        else:
            pl.when(flag)(run)

    def chain_copy(which, number):
        buf = bufs[which]
        (f0, a0), (f1, a1), device, sent, _ = route(which, number)
        group = 0 if sent is None else 1 if sent is has_out else 2
        return remote(
            buf.at[f0, a0, pl.ds(0, 2)], buf.at[f1, a1, pl.ds(0, 2)],
            chain_send.at[group, which], chain_recv.at[number - 1, which], device,
        )

    def across_copy(which, f, a):
        buf = bufs[which]
        return remote(
            buf.at[f, a, 1], buf.at[f, a, 2], across_send.at[f, which], across_recv.at[f * 3 + a, which], other_core
        )

    def fin_parts(which, n):
        dst = (out_ref, gq_ref, gk_ref, gv_ref)[which]
        return (
            results.at[which, pl.ds(n * TILE, TILE), :],
            dst.at[:, pl.ds(pl.multiple_of(col * HD, HD), HD)],
        )

    def fin_copy(which, n):
        src, dst = fin_parts(which, n)
        return remote(src, dst, fin_send.at[n, which], fin_recv.at[col, which], owner(n))

    def send_fin(which):
        for n in range(4):
            mine = owner(n) == place

            @pl.when(mine)
            def _():
                src, dst = fin_parts(which, n)
                pltpu.make_async_copy(src, dst, fin_recv.at[col, which]).start()

            @pl.when(jnp.logical_not(mine))
            def _():
                fin_copy(which, n).start()

    def exists(f):
        return (None, has_out, has_in)[f]

    pltpu.make_async_copy(win_hbm, win_ref, win_sem).wait()

    @pl.when(active)
    def _():
        at_head = jnp.minimum(col, HEADS_HERE - 1)
        win_t = win_ref[at_head, 0]
        win_h = win_ref[at_head, 1]
        win_w = win_ref[at_head, 2]

        def bias(f, a, b, first, count):
            q_tile = lax.broadcasted_iota(jnp.int32, (1, count), 1) // TILE + first // TILE
            q_lh = q_tile // 2
            q_lw = ((q_tile + 1) // 2) % 2
            bad = jnp.maximum(jnp.abs(q_lh - a) - win_h, jnp.abs(q_lw - b) - win_w)
            if f != HERE:
                bad = jnp.maximum(bad, 1 - win_t)
            return jnp.where(bad > 0, -jnp.inf, 0.0).astype(F32)

        def score_row(f, a):
            def run():
                for b, first, count in blocks(a):
                    lanes = slice(first, first + count)
                    s = dot_nt(kbuf[f, a, b], q_own[lanes, :]) + bias(f, a, b, first, count)
                    s_buf[f * 3 + a, b * TILE : (b + 1) * TILE, lanes] = s
                    top_ref[:, lanes] = jnp.maximum(
                        top_ref[:, lanes], jnp.max(s.reshape(TILE // 8, 8, count), axis=0)
                    )

            only(exists(f), run)

        def exp_row(f, a):
            def run():
                for b, first, count in blocks(a):
                    lanes = slice(first, first + count)
                    keys = slice(b * TILE, (b + 1) * TILE)
                    e = jnp.exp2((s_buf[f * 3 + a, keys, lanes] - top_ref[:1, lanes]) * EXP2_SCALE)
                    s_buf[f * 3 + a, keys, lanes] = e
                    sum_ref[:, lanes] += jnp.sum(e.reshape(TILE // 8, 8, count), axis=0)

            only(exists(f), run)

        def v_row(f, a):
            def run():
                for b, first, count in blocks(a):
                    lanes = slice(first, first + count)
                    keys = slice(b * TILE, (b + 1) * TILE)
                    p = s_buf[f * 3 + a, keys, lanes] * sum_ref[:1, lanes]
                    s_buf[f * 3 + a, keys, lanes] = p
                    p_low[keys, lanes] = p.astype(BF16)
                    dp_buf[f * 3 + a, keys, lanes] = dot_nt(vbuf[f, a, b], g_own[lanes, :])
                for b, n, first, count in pieces(a):
                    lanes = slice(first, first + count)
                    keys = slice(b * TILE, (b + n) * TILE)
                    vals = vbuf[f, a, b : b + n].reshape(n * TILE, HD)
                    out_t[:, lanes] += dot_tn(vals, p_low[keys, lanes])

            only(exists(f), run)

        def dq_row(f, a):
            def run():
                for b, first, count in blocks(a):
                    lanes = slice(first, first + count)
                    keys = slice(b * TILE, (b + 1) * TILE)
                    ds = s_buf[f * 3 + a, keys, lanes] * (dp_buf[f * 3 + a, keys, lanes] - top_ref[:1, lanes])
                    ds_low[keys, lanes] = ds.astype(BF16)
                for b, n, first, count in pieces(a):
                    lanes = slice(first, first + count)
                    keys = slice(b * TILE, (b + n) * TILE)
                    vals = kbuf[f, a, b : b + n].reshape(n * TILE, HD)
                    gq_t[:, lanes] += dot_tn(vals, ds_low[keys, lanes])

            only(exists(f), run)

        def kv_row(f, a):
            def run():
                for b, first, count in blocks(a):
                    lanes = slice(first, first + count)
                    rows = slice(b * TILE, (b + 1) * TILE)
                    of_query = stats[f, a, b].T
                    top, inverse, delta = of_query[:, 0:1], of_query[:, 1:2], of_query[:, 2:3]
                    s = dot_nt(qbuf[f, a, b], k_own[lanes, :]) + bias(f, a, b, first, count)
                    p = jnp.exp2((s - top) * EXP2_SCALE) * inverse
                    p_low[rows, lanes] = p.astype(BF16)
                    dp = dot_nt(gbuf[f, a, b], v_own[lanes, :])
                    ds_low[rows, lanes] = (p * (dp - delta)).astype(BF16)
                for b, n, first, count in pieces(a):
                    lanes = slice(first, first + count)
                    rows = slice(b * TILE, (b + n) * TILE)
                    gv_t[:, lanes] += dot_tn(gbuf[f, a, b : b + n].reshape(n * TILE, HD), p_low[rows, lanes])
                    gk_t[:, lanes] += dot_tn(qbuf[f, a, b : b + n].reshape(n * TILE, HD), ds_low[rows, lanes])

            only(exists(f), run)

        def chain_go(which, *numbers):
            for number in numbers:
                only(route(which, number)[3], lambda: chain_copy(which, number).start())

        def chain_arrive(which, number):
            def run():
                chain_copy(which, number).wait_recv()
                across_copy(which, *route(which, number)[1]).start()

            only(route(which, number)[4], run)

        def across_arrive(which, f, a):
            only(exists(f), lambda: across_copy(which, f, a).wait_recv())

        def own_arrive(which, a):
            wait_for(bufs[which].at[HERE, a, pl.ds(0, 2)], own_recv.at[a, which])
            across_copy(which, HERE, a).start()

        def keep_own(which):
            for n in range(4):
                own[which][n * TILE : (n + 1) * TILE, :] = bufs[which][HERE, OWN[n][0], OWN[n][1]]

        def gather_first(which):
            own_arrive(which, 1)
            chain_go(which, 1, 2)
            own_arrive(which, 0)

        def gather_second(which):
            chain_arrive(which, 1)
            chain_go(which, 3)
            chain_arrive(which, 2)
            chain_go(which, 6)

        def gather_third(which):
            chain_arrive(which, 3)
            chain_go(which, 7)

        def gather_rest(which):
            def far_arrive(side):
                f = (OUT, IN)[side]
                wait_for(bufs[which].at[f, 0, pl.ds(0, 2)], far_recv.at[side, which])
                across_copy(which, f, 0).start()

            pl.when(has_out)(lambda: far_arrive(0))
            pl.when(has_in)(lambda: far_arrive(1))
            for number in (6, 7):
                chain_arrive(which, number)

        def all_lanes(value):
            return jnp.broadcast_to(value, (8, Q_ALL))

        gather_first(K)
        own_arrive(Q, 1)
        own_arrive(Q, 0)
        keep_own(Q)
        for which in (K, Q, V):
            own_left(which)
        send_far(K)
        gather_first(V)
        send_far(V)
        top_ref[...] = jnp.full((8, Q_ALL), -jnp.inf, F32)
        for a in (0, 1):
            across_arrive(K, HERE, a)
            score_row(HERE, a)
        gather_second(K)
        gather_second(V)
        chain_go(Q, 1, 2)
        across_arrive(K, HERE, 2)
        score_row(HERE, 2)
        across_arrive(K, OUT, 2)
        score_row(OUT, 2)
        gather_third(K)
        gather_third(V)
        gather_first(G)
        own_left(G)
        across_arrive(K, OUT, 1)
        score_row(OUT, 1)
        gather_rest(K)
        gather_second(Q)
        send_far(Q)
        across_arrive(K, OUT, 0)
        score_row(OUT, 0)
        for a in range(3):
            across_arrive(K, IN, a)
            score_row(IN, a)
        gather_second(G)
        send_far(G)
        for which in (K, V, G):
            keep_own(which)
        top_ref[...] = all_lanes(jnp.max(top_ref[...], axis=0, keepdims=True))
        stats[HERE, :2, :2] = jnp.zeros((2, 2, 8, TILE), F32)
        for n, (a, b) in enumerate(OWN):
            stats[HERE, a, b, 0:1, :] = top_ref[:1, n * TILE : (n + 1) * TILE]
        sum_ref[...] = jnp.zeros((8, Q_ALL), F32)
        for ref in (out_t, gq_t, gk_t, gv_t):
            ref[...] = jnp.zeros((HD, Q_ALL), F32)
        for f in range(3):
            for a in range(3):
                exp_row(f, a)
        sum_ref[...] = all_lanes(1.0 / jnp.sum(sum_ref[...], axis=0, keepdims=True))
        for n, (a, b) in enumerate(OWN):
            stats[HERE, a, b, 1:2, :] = sum_ref[:1, n * TILE : (n + 1) * TILE]
        gather_third(Q)
        for f, a in ((HERE, 0), (HERE, 1), (HERE, 2), (OUT, 2), (OUT, 1)):
            across_arrive(V, f, a)
            v_row(f, a)
        gather_third(G)
        gather_rest(V)
        for f, a in ((OUT, 0), (IN, 0), (IN, 1), (IN, 2)):
            across_arrive(V, f, a)
            v_row(f, a)
        for n, (a, b) in enumerate(OWN):
            lanes = slice(n * TILE, (n + 1) * TILE)
            o_t = out_t[:, lanes]
            g_t = g_own[lanes, :].astype(F32).T
            delta = jnp.sum(o_t * g_t, axis=0, keepdims=True)
            top_ref[:, lanes] = jnp.broadcast_to(delta, (8, TILE))
            stats[HERE, a, b, 2:3, :] = delta
        chain_go(STATS, 7, 3, 6, 4, 5, 2, 1)
        across_copy(STATS, HERE, 1).start()
        across_copy(STATS, HERE, 0).start()

        def give(which, total, factor):
            for n in range(4):
                lanes = slice(n * TILE, (n + 1) * TILE)
                results[which, lanes, :] = (total[:, lanes] * factor).T.astype(BF16)
            send_fin(which)

        give(0, out_t, 1.0)
        for a in range(3):
            dq_row(HERE, a)
        for a in range(2):
            for which in (Q, G, STATS):
                across_arrive(which, HERE, a)
            kv_row(HERE, a)
        gather_rest(Q)
        for a in range(3):
            dq_row(OUT, a)
        gather_rest(G)
        for a in range(3):
            dq_row(IN, a)
        for number in range(1, 8):
            chain_arrive(STATS, number)
        give(1, gq_t, SCALE)
        for f, a in ((HERE, 2), (OUT, 2), (OUT, 1), (OUT, 0), (IN, 0), (IN, 1), (IN, 2)):
            for which in (Q, G, STATS):
                across_arrive(which, f, a)
            kv_row(f, a)
        give(2, gk_t, SCALE)
        give(3, gv_t, 1.0)

    for head in range(HEADS_HERE):
        for which, ref in enumerate((out_ref, gq_ref, gk_ref, gv_ref)):
            wait_for(ref.at[:, pl.ds(head * HD, HD)], fin_recv.at[head, which])

    for which in range(4):
        for side in range(2):
            @pl.when(jnp.logical_and(at_edge, far_flag[side]))
            def _():
                wait_for(inputs[which], far_send.at[side, which])

    @pl.when(active)
    def _():
        for which in range(5):
            buf = bufs[which]
            wait_for(buf.at[HERE, 0, pl.ds(0, 2)], chain_send.at[0, which])
            if which == STATS:
                three = buf.at[HERE, pl.ds(0, 3), pl.ds(0, 2)]
                only(has_out, lambda: wait_for(three, chain_send.at[1, which]))
                only(has_in, lambda: wait_for(three, chain_send.at[2, which]))
            else:
                four = buf.at[pl.ds(0, 2), pl.ds(0, 2), pl.ds(0, 2)]
                only(has_out, lambda: wait_for(four, chain_send.at[1, which]))
            for f in range(3):
                only(exists(f), lambda: wait_for(buf.at[f, 0], across_send.at[f, which]))
        for n in range(4):
            @pl.when(owner(n) != place)
            def _():
                for which in range(4):
                    fin_copy(which, n).wait_send()


def body(queries, keys, values, grad_out, head_window):
    shape = jax.ShapeDtypeStruct((TILE, HEADS_HERE * HD), BF16)
    hbm = pl.BlockSpec(memory_space=pltpu.HBM)
    dma = pltpu.SemaphoreType.DMA
    return pl.pallas_call(
        kernel,
        out_shape=(shape,) * 4,
        in_specs=[hbm] * 5,
        out_specs=(hbm,) * 4,
        scratch_shapes=[
            pltpu.VMEM((3, 3, 3, TILE, HD), BF16),
            pltpu.VMEM((3, 3, 3, TILE, HD), BF16),
            pltpu.VMEM((3, 3, 3, TILE, HD), BF16),
            pltpu.VMEM((3, 3, 3, TILE, HD), BF16),
            pltpu.VMEM((3, 3, 3, 8, TILE), F32),
            pltpu.VMEM((Q_ALL, HD), BF16),
            pltpu.VMEM((Q_ALL, HD), BF16),
            pltpu.VMEM((Q_ALL, HD), BF16),
            pltpu.VMEM((Q_ALL, HD), BF16),
            pltpu.VMEM((ROWS, 3 * TILE, Q_ALL), F32),
            pltpu.VMEM((ROWS, 3 * TILE, Q_ALL), F32),
            pltpu.VMEM((3 * TILE, Q_ALL), BF16),
            pltpu.VMEM((3 * TILE, Q_ALL), BF16),
            pltpu.VMEM((8, Q_ALL), F32),
            pltpu.VMEM((8, Q_ALL), F32),
            pltpu.VMEM((HD, Q_ALL), F32),
            pltpu.VMEM((HD, Q_ALL), F32),
            pltpu.VMEM((HD, Q_ALL), F32),
            pltpu.VMEM((HD, Q_ALL), F32),
            pltpu.VMEM((4, Q_ALL, HD), BF16),
            pltpu.SMEM((HEADS_HERE, 3), jnp.int32),
            dma((4,)),
            dma((2, 4)),
            dma((2, 4)),
            dma((2, 4)),
            dma((3, 5)),
            dma((7, 5)),
            dma((3, 5)),
            dma((9, 5)),
            dma((4, 4)),
            dma((3, 4)),
            dma,
        ],
        compiler_params=pltpu.CompilerParams(
            collective_id=0, has_side_effects=True, vmem_limit_bytes=48 * 1024 * 1024
        ),
    )(queries, keys, values, grad_out, head_window)


def solution(mesh):
    in_specs = (P("st", "hd"), P("st", "hd"), P("st", "hd"), P("st", "hd"), P("hd", None))
    out_specs = (P("st", "hd"), P("st", "hd"), P("st", "hd"), P("st", "hd"))
    return jax.shard_map(body, mesh=mesh, in_specs=in_specs, out_specs=out_specs, check_vma=False)
```

```python
import functools
import math

import jax
import jax.numpy as jnp
from jax import lax
from jax.experimental import pallas as pl
from jax.experimental.pallas import tpu as pltpu
from jax.sharding import PartitionSpec as P

HD = 128
TILE = 128
FRAMES = 4
HEADS_HERE = 3
SCALE = HD ** (-0.5)
EXP2_SCALE = SCALE * math.log2(math.e)
MESH = pl.DeviceIdType.MESH
BF16 = jnp.bfloat16
F32 = jnp.float32

OWN = ((0, 0), (0, 1), (1, 1), (1, 0))
HERE, OUT, IN = 0, 1, 2
ROWS = 9
K, V, Q, G, STATS = range(5)
Q_ALL = 4 * TILE


def blocks(lh):
    if lh < 2:
        return ((0, 0, 4 * TILE), (1, 0, 4 * TILE), (2, TILE, 2 * TILE))
    return ((0, 2 * TILE, 2 * TILE), (1, 2 * TILE, 2 * TILE), (2, 2 * TILE, TILE))


def pieces(lh):
    if lh < 2:
        return ((0, 2, 0, 4 * TILE), (2, 1, TILE, 2 * TILE))
    return ((0, 2, 2 * TILE, 2 * TILE), (2, 1, 2 * TILE, TILE))


def dot_nt(a, b):
    return lax.dot_general(a, b, (((1,), (1,)), ((), ())), preferred_element_type=F32)


def dot_tn(a, b):
    return lax.dot_general(a, b, (((0,), (0,)), ((), ())), preferred_element_type=F32)


def dot_nn(a, b):
    return lax.dot_general(a, b, (((1,), (0,)), ((), ())), preferred_element_type=F32)


def kernel(
    q_ref, k_ref, v_ref, g_ref, win_hbm,
    out_ref, gq_ref, gk_ref, gv_ref,
    kbuf, vbuf, qbuf, gbuf, stats, k_own, v_own, q_own, g_own, s_buf, dp_buf, p_low, ds_low, top_ref, sum_ref,
    out_t, gq_t, gk_t, gv_t, results, win_ref,
    own_send, own_recv, far_send, far_recv, chain_send, chain_recv, across_send, across_recv,
    fin_send, fin_recv, win_sem,
):
    pltpu.make_async_copy(win_hbm, win_ref, win_sem).start()
    inputs = (k_ref, v_ref, q_ref, g_ref)
    bufs = (kbuf, vbuf, qbuf, gbuf, stats)
    own = (k_own, v_own, q_own, g_own)
    place = lax.axis_index("st")
    t = place // 16
    upper = (place // 8) % 2
    col = (place // 2) % 4
    core = place % 2
    active = col < HEADS_HERE
    row = (place // 4) % 4
    column = place % 4
    w_half = column // 2
    lh_own = (row + upper) % 2
    lw_own = (column + w_half) % 2
    is_self = jnp.logical_and(active, w_half == core)
    outward = 2 * upper - 1
    t_out = t + outward
    t_in = t - outward
    has_out = jnp.logical_and(t_out >= 0, t_out < FRAMES)
    has_in = jnp.logical_and(t_in >= 0, t_in < FRAMES)
    other_core = place + 1 - 2 * core
    mate = place - 8 * outward
    outer = place + 8 * outward
    out2 = place + 16 * outward
    in2 = place - 16 * outward
    in3 = place - 24 * outward

    def worker(head):
        return (2 * t + upper) * 8 + 2 * head + w_half

    def owner(n):
        a, b = OWN[n]
        r = upper * (3 - a) + (1 - upper) * a
        c = core * (3 - b) + (1 - core) * b
        return t * 16 + r * 4 + c

    def far_owner(n, frame):
        a, b = OWN[n]
        r = upper * (3 - a) + (1 - upper) * a
        c = core * (3 - b) + (1 - core) * b
        return frame * 16 + r * 4 + c

    def remote(src, dst, send, recv, device):
        return pltpu.make_async_remote_copy(
            src_ref=src, dst_ref=dst, send_sem=send, recv_sem=recv,
            device_id={"st": device}, device_id_type=MESH,
        )

    def wait_for(dst, sem):
        pltpu.make_async_copy(dst, dst, sem).wait()

    barrier = pltpu.get_barrier_semaphore()

    def greet(device):
        pl.semaphore_signal(barrier, inc=1, device_id={"st": device}, device_id_type=MESH)

    at_edge = lh_own == 0

    def far_worker(side, head):
        return worker(head) + (-16, 16)[side] * outward

    far_flag = (has_in, has_out)
    for head in range(HEADS_HERE):
        @pl.when(worker(head) != place)
        def _():
            greet(worker(head))

        for side in range(2):
            @pl.when(jnp.logical_and(at_edge, far_flag[side]))
            def _():
                greet(far_worker(side, head))

    @pl.when(active)
    def _():
        for n in range(4):
            @pl.when(owner(n) != place)
            def _():
                greet(owner(n))

        greet(other_core)
        greet(mate)

        @pl.when(has_out)
        def _():
            greet(outer)
            greet(out2)
            for n in range(2):
                greet(far_owner(n, t_out))

        @pl.when(has_in)
        def _():
            greet(in2)
            greet(in3)
            for n in range(2):
                greet(far_owner(n, t_in))

    as_int = lambda flag: flag.astype(jnp.int32)
    selfs = as_int(is_self)
    greeted = 3 - selfs + 3 * as_int(at_edge) * (as_int(has_in) + as_int(has_out))
    pl.semaphore_wait(
        barrier, greeted + as_int(active) * (6 - selfs + 4 * as_int(has_out) + 4 * as_int(has_in))
    )

    def head_cols(ref, head):
        return ref.at[:, pl.ds(head * HD, HD)]

    def own_copy(which, head):
        return remote(
            head_cols(inputs[which], head), bufs[which].at[HERE, lh_own, lw_own],
            own_send.at[which], own_recv.at[lh_own, which], worker(head),
        )

    def far_copy(which, side, head):
        return remote(
            head_cols(inputs[which], head), bufs[which].at[(OUT, IN)[side], 0, lw_own],
            far_send.at[side, which], far_recv.at[side, which], far_worker(side, head),
        )

    def send_own(which):
        for head in range(HEADS_HERE):
            mine = worker(head) == place

            @pl.when(mine)
            def _():
                pltpu.make_async_copy(
                    head_cols(inputs[which], head), bufs[which].at[HERE, lh_own, lw_own], own_recv.at[lh_own, which]
                ).start()

            @pl.when(jnp.logical_not(mine))
            def _():
                own_copy(which, head).start()

    def own_left(which):
        ref = inputs[which]

        @pl.when(is_self)
        def _():
            wait_for(ref.at[:, pl.ds(0, (HEADS_HERE - 1) * HD)], own_send.at[which])

        @pl.when(jnp.logical_not(is_self))
        def _():
            wait_for(ref, own_send.at[which])

    def by_chain_at(head, half):
        if isinstance(head, int):
            low = jnp.logical_and(upper == 0, half == 0) if head == 2 else half < 0
            high = jnp.logical_and(upper == 1, half == head) if head < 2 else half < 0
            return jnp.logical_or(low, high)
        low = (upper == 0) & (half == 0) & (head == 2)
        return low | ((upper == 1) & (half == head) & (head < 2))

    by_chain = by_chain_at(col, core)
    skips = jnp.logical_or(upper == 1, w_half == 0)

    def send_far(which):
        for side in range(2):
            @pl.when(jnp.logical_and(at_edge, far_flag[side]))
            def _():
                for head in range(HEADS_HERE):
                    @pl.when(jnp.logical_not(by_chain_at(head, w_half)))
                    def _():
                        far_copy(which, side, head).start()

    for which in (K, Q, V, G):
        send_own(which)

    @pl.when(jnp.logical_not(active))
    def _():
        for which in (K, Q, V, G):
            own_left(which)
        for which in (K, V, Q, G):
            send_far(which)

    CHAIN = {
        1: ((HERE, 1), (HERE, 2), mate, None, None),
        2: ((HERE, 1), (OUT, 2), outer, has_out, has_out),
        3: ((HERE, 2), (OUT, 1), outer, has_out, has_out),
        4: ((HERE, 0), (OUT, 0), in2, has_in, has_out),
        5: ((HERE, 0), (IN, 0), out2, has_out, has_in),
        6: ((OUT, 2), (IN, 1), mate, has_out, has_in),
        7: ((OUT, 1), (IN, 2), mate, has_out, has_in),
    }
    STATS_TO = {
        1: CHAIN[1],
        2: CHAIN[2],
        3: ((HERE, 1), (OUT, 1), in2, has_in, has_out),
        4: CHAIN[4],
        5: CHAIN[5],
        6: ((HERE, 1), (IN, 1), out2, has_out, has_in),
        7: ((HERE, 1), (IN, 2), in3, has_in, has_in),
    }

    def route(which, number):
        return (STATS_TO if which == STATS else CHAIN)[number]

    def send_group(which, number):
        sent = route(which, number)[3]
        if number == 5 and which != STATS:
            return 3
        return 0 if sent is None else 1 if sent is has_out else 2

    def routes_of(which):
        return (1, 2, 3, 6, 7) if which != STATS else (1, 2, 3, 4, 5, 6, 7)

    def only(flag, run):
        if flag is None:
            run()
        else:
            pl.when(flag)(run)

    def chain_copy(which, number):
        buf = bufs[which]
        (f0, a0), (f1, a1), device, _, _ = route(which, number)
        return remote(
            buf.at[f0, a0, pl.ds(0, 2)], buf.at[f1, a1, pl.ds(0, 2)],
            chain_send.at[send_group(which, number), which], chain_recv.at[number - 1, which], device,
        )

    def across_copy(which, f, a):
        buf = bufs[which]
        return remote(
            buf.at[f, a, 1], buf.at[f, a, 2], across_send.at[f, which], across_recv.at[f * 3 + a, which], other_core
        )

    def fin_parts(which, n):
        dst = (out_ref, gq_ref, gk_ref, gv_ref)[which]
        return (
            results.at[which, pl.ds(n * TILE, TILE), :],
            dst.at[:, pl.ds(pl.multiple_of(col * HD, HD), HD)],
        )

    def fin_copy(which, n):
        src, dst = fin_parts(which, n)
        return remote(src, dst, fin_send.at[n, which], fin_recv.at[col, which], owner(n))

    def send_fin(which):
        for n in range(4):
            mine = owner(n) == place

            @pl.when(mine)
            def _():
                src, dst = fin_parts(which, n)
                pltpu.make_async_copy(src, dst, fin_recv.at[col, which]).start()

            @pl.when(jnp.logical_not(mine))
            def _():
                fin_copy(which, n).start()

    def exists(f):
        return (None, has_out, has_in)[f]

    pltpu.make_async_copy(win_hbm, win_ref, win_sem).wait()

    @pl.when(active)
    def _():
        at_head = jnp.minimum(col, HEADS_HERE - 1)
        win_t = win_ref[at_head, 0]
        win_h = win_ref[at_head, 1]
        win_w = win_ref[at_head, 2]

        def bias(f, a, b, first, count):
            q_tile = lax.broadcasted_iota(jnp.int32, (1, count), 1) // TILE + first // TILE
            q_lh = q_tile // 2
            q_lw = ((q_tile + 1) // 2) % 2
            bad = jnp.maximum(jnp.abs(q_lh - a) - win_h, jnp.abs(q_lw - b) - win_w)
            if f != HERE:
                bad = jnp.maximum(bad, 1 - win_t)
            return jnp.where(bad > 0, -jnp.inf, 0.0).astype(F32)

        def score_row(f, a):
            def run():
                for b, first, count in blocks(a):
                    lanes = slice(first, first + count)
                    s = dot_nt(kbuf[f, a, b], q_own[lanes, :]) + bias(f, a, b, first, count)
                    s_buf[f * 3 + a, b * TILE : (b + 1) * TILE, lanes] = s
                    top_ref[:, lanes] = jnp.maximum(
                        top_ref[:, lanes], jnp.max(s.reshape(TILE // 8, 8, count), axis=0)
                    )

            only(exists(f), run)

        def exp_row(f, a):
            def run():
                for b, first, count in blocks(a):
                    lanes = slice(first, first + count)
                    keys = slice(b * TILE, (b + 1) * TILE)
                    e = jnp.exp2((s_buf[f * 3 + a, keys, lanes] - top_ref[:1, lanes]) * EXP2_SCALE)
                    s_buf[f * 3 + a, keys, lanes] = e
                    sum_ref[:, lanes] += jnp.sum(e.reshape(TILE // 8, 8, count), axis=0)

            only(exists(f), run)

        def v_row(f, a):
            def run():
                for b, first, count in blocks(a):
                    lanes = slice(first, first + count)
                    keys = slice(b * TILE, (b + 1) * TILE)
                    p = s_buf[f * 3 + a, keys, lanes] * sum_ref[:1, lanes]
                    s_buf[f * 3 + a, keys, lanes] = p
                    p_low[keys, lanes] = p.astype(BF16)
                    dp_buf[f * 3 + a, keys, lanes] = dot_nt(vbuf[f, a, b], g_own[lanes, :])
                for b, n, first, count in pieces(a):
                    lanes = slice(first, first + count)
                    keys = slice(b * TILE, (b + n) * TILE)
                    vals = vbuf[f, a, b : b + n].reshape(n * TILE, HD)
                    out_t[:, lanes] += dot_tn(vals, p_low[keys, lanes])

            only(exists(f), run)

        def dq_row(f, a):
            def run():
                for b, first, count in blocks(a):
                    lanes = slice(first, first + count)
                    keys = slice(b * TILE, (b + 1) * TILE)
                    ds = s_buf[f * 3 + a, keys, lanes] * (dp_buf[f * 3 + a, keys, lanes] - top_ref[:1, lanes])
                    ds_low[keys, lanes] = ds.astype(BF16)
                for b, n, first, count in pieces(a):
                    lanes = slice(first, first + count)
                    keys = slice(b * TILE, (b + n) * TILE)
                    vals = kbuf[f, a, b : b + n].reshape(n * TILE, HD)
                    gq_t[:, lanes] += dot_tn(vals, ds_low[keys, lanes])

            only(exists(f), run)

        def kv_row(f, a):
            def run():
                for b, first, count in blocks(a):
                    lanes = slice(first, first + count)
                    rows = slice(b * TILE, (b + 1) * TILE)
                    of_query = stats[f, a, b].T
                    top, inverse, delta = of_query[:, 0:1], of_query[:, 1:2], of_query[:, 2:3]
                    s = dot_nt(qbuf[f, a, b], k_own[lanes, :]) + bias(f, a, b, first, count)
                    p = jnp.exp2((s - top) * EXP2_SCALE) * inverse
                    p_low[rows, lanes] = p.astype(BF16)
                    dp = dot_nt(gbuf[f, a, b], v_own[lanes, :])
                    ds_low[rows, lanes] = (p * (dp - delta)).astype(BF16)
                for b, n, first, count in pieces(a):
                    lanes = slice(first, first + count)
                    rows = slice(b * TILE, (b + n) * TILE)
                    gv_t[:, lanes] += dot_tn(gbuf[f, a, b : b + n].reshape(n * TILE, HD), p_low[rows, lanes])
                    gk_t[:, lanes] += dot_tn(qbuf[f, a, b : b + n].reshape(n * TILE, HD), ds_low[rows, lanes])

            only(exists(f), run)

        def chain_go(which, *numbers):
            for number in numbers:
                only(route(which, number)[3], lambda: chain_copy(which, number).start())

        def chain_arrive(which, number):
            def run():
                chain_copy(which, number).wait_recv()
                across_copy(which, *route(which, number)[1]).start()

            only(route(which, number)[4], run)

        def across_arrive(which, f, a):
            only(exists(f), lambda: across_copy(which, f, a).wait_recv())

        def own_arrive(which, a):
            wait_for(bufs[which].at[HERE, a, pl.ds(0, 2)], own_recv.at[a, which])
            across_copy(which, HERE, a).start()

        def keep_own(which):
            for n in range(4):
                own[which][n * TILE : (n + 1) * TILE, :] = bufs[which][HERE, OWN[n][0], OWN[n][1]]

        def gather_first(which):
            own_arrive(which, 1)
            chain_go(which, 1, 2)
            own_arrive(which, 0)

        def gather_second(which):
            chain_arrive(which, 1)
            chain_go(which, 3)
            chain_arrive(which, 2)
            chain_go(which, 6)

        def gather_third(which):
            chain_arrive(which, 3)
            chain_go(which, 7)

        def gather_rest(which):
            def far_arrive(side):
                f = (OUT, IN)[side]

                @pl.when(by_chain)
                def _():
                    chain_copy(which, 4 + side).wait_recv()

                @pl.when(jnp.logical_not(by_chain))
                def _():
                    wait_for(bufs[which].at[f, 0, pl.ds(0, 2)], far_recv.at[side, which])

                across_copy(which, f, 0).start()

            pl.when(has_out)(lambda: far_arrive(0))
            pl.when(has_in)(lambda: far_arrive(1))
            for number in (6, 7):
                chain_arrive(which, number)

        def all_lanes(value):
            return jnp.broadcast_to(value, (8, Q_ALL))

        def go_far(which):
            send_far(which)

            @pl.when(by_chain)
            def _():
                chain_go(which, 4, 5)

        gather_first(K)
        own_arrive(Q, 1)
        own_arrive(Q, 0)
        keep_own(Q)
        for which in (K, Q, V):
            own_left(which)
        go_far(K)
        gather_first(V)
        go_far(V)
        top_ref[...] = jnp.full((8, Q_ALL), -jnp.inf, F32)
        for a in (0, 1):
            across_arrive(K, HERE, a)
            score_row(HERE, a)
        gather_second(K)
        gather_second(V)
        chain_go(Q, 1, 2)
        across_arrive(K, HERE, 2)
        score_row(HERE, 2)
        across_arrive(K, OUT, 2)
        score_row(OUT, 2)
        gather_third(K)
        gather_third(V)
        gather_first(G)
        own_left(G)
        across_arrive(K, OUT, 1)
        score_row(OUT, 1)
        gather_rest(K)
        gather_second(Q)
        go_far(Q)
        across_arrive(K, OUT, 0)
        score_row(OUT, 0)
        for a in range(3):
            across_arrive(K, IN, a)
            score_row(IN, a)
        gather_second(G)
        go_far(G)
        for which in (K, V, G):
            keep_own(which)
        top_ref[...] = all_lanes(jnp.max(top_ref[...], axis=0, keepdims=True))
        stats[HERE, :2, :2] = jnp.zeros((2, 2, 8, TILE), F32)
        for n, (a, b) in enumerate(OWN):
            stats[HERE, a, b, 0:1, :] = top_ref[:1, n * TILE : (n + 1) * TILE]
        sum_ref[...] = jnp.zeros((8, Q_ALL), F32)
        for ref in (out_t, gq_t, gk_t, gv_t):
            ref[...] = jnp.zeros((HD, Q_ALL), F32)
        for f in range(3):
            for a in range(3):
                exp_row(f, a)
        sum_ref[...] = all_lanes(1.0 / jnp.sum(sum_ref[...], axis=0, keepdims=True))
        for n, (a, b) in enumerate(OWN):
            stats[HERE, a, b, 1:2, :] = sum_ref[:1, n * TILE : (n + 1) * TILE]
        gather_third(Q)
        for f, a in ((HERE, 0), (HERE, 1), (HERE, 2), (OUT, 2), (OUT, 1)):
            across_arrive(V, f, a)
            v_row(f, a)
        gather_third(G)
        gather_rest(V)
        for f, a in ((OUT, 0), (IN, 0), (IN, 1), (IN, 2)):
            across_arrive(V, f, a)
            v_row(f, a)
        for n, (a, b) in enumerate(OWN):
            lanes = slice(n * TILE, (n + 1) * TILE)
            o_t = out_t[:, lanes]
            g_t = g_own[lanes, :].astype(F32).T
            delta = jnp.sum(o_t * g_t, axis=0, keepdims=True)
            top_ref[:, lanes] = jnp.broadcast_to(delta, (8, TILE))
            stats[HERE, a, b, 2:3, :] = delta
        chain_go(STATS, 7, 3, 6, 4, 5, 2, 1)
        across_copy(STATS, HERE, 1).start()
        across_copy(STATS, HERE, 0).start()

        def give(which, total, factor):
            for n in range(4):
                lanes = slice(n * TILE, (n + 1) * TILE)
                results[which, lanes, :] = (total[:, lanes] * factor).T.astype(BF16)
            send_fin(which)

        give(0, out_t, 1.0)
        for a in range(3):
            dq_row(HERE, a)
        for a in range(2):
            for which in (Q, G, STATS):
                across_arrive(which, HERE, a)
            kv_row(HERE, a)
        gather_rest(Q)
        for a in range(3):
            dq_row(OUT, a)
        gather_rest(G)
        for a in range(3):
            dq_row(IN, a)
        for number in range(1, 8):
            chain_arrive(STATS, number)
        give(1, gq_t, SCALE)
        for f, a in ((HERE, 2), (OUT, 2), (OUT, 1), (OUT, 0), (IN, 0), (IN, 1), (IN, 2)):
            for which in (Q, G, STATS):
                across_arrive(which, f, a)
            kv_row(f, a)
        give(2, gk_t, SCALE)
        give(3, gv_t, 1.0)

    for head in range(HEADS_HERE):
        for which, ref in enumerate((out_ref, gq_ref, gk_ref, gv_ref)):
            wait_for(ref.at[:, pl.ds(head * HD, HD)], fin_recv.at[head, which])

    for which in range(4):
        for side in range(2):
            sends = jnp.logical_and(at_edge, far_flag[side])

            @pl.when(jnp.logical_and(sends, skips))
            def _():
                wait_for(inputs[which].at[:, pl.ds(0, (HEADS_HERE - 1) * HD)], far_send.at[side, which])

            @pl.when(jnp.logical_and(sends, jnp.logical_not(skips)))
            def _():
                wait_for(inputs[which], far_send.at[side, which])

    @pl.when(active)
    def _():
        for which in range(5):
            buf = bufs[which]
            for group in range(4):
                numbers = [x for x in routes_of(which) if send_group(which, x) == group]
                if numbers:
                    if len(numbers) == 4:
                        rows = buf.at[pl.ds(0, 2), pl.ds(0, 2), pl.ds(0, 2)]
                    else:
                        rows = buf.at[HERE, pl.ds(0, len(numbers)), pl.ds(0, 2)]
                    only(route(which, numbers[0])[3], lambda: wait_for(rows, chain_send.at[group, which]))
            if which != STATS:
                for number in (4, 5):
                    @pl.when(jnp.logical_and(by_chain, CHAIN[number][3]))
                    def _():
                        chain_copy(which, number).wait_send()

            for f in range(3):
                only(exists(f), lambda: wait_for(buf.at[f, 0], across_send.at[f, which]))
        for n in range(4):
            @pl.when(owner(n) != place)
            def _():
                for which in range(4):
                    fin_copy(which, n).wait_send()


def body(queries, keys, values, grad_out, head_window):
    shape = jax.ShapeDtypeStruct((TILE, HEADS_HERE * HD), BF16)
    hbm = pl.BlockSpec(memory_space=pltpu.HBM)
    dma = pltpu.SemaphoreType.DMA
    return pl.pallas_call(
        kernel,
        out_shape=(shape,) * 4,
        in_specs=[hbm] * 5,
        out_specs=(hbm,) * 4,
        scratch_shapes=[
            pltpu.VMEM((3, 3, 3, TILE, HD), BF16),
            pltpu.VMEM((3, 3, 3, TILE, HD), BF16),
            pltpu.VMEM((3, 3, 3, TILE, HD), BF16),
            pltpu.VMEM((3, 3, 3, TILE, HD), BF16),
            pltpu.VMEM((3, 3, 3, 8, TILE), F32),
            pltpu.VMEM((Q_ALL, HD), BF16),
            pltpu.VMEM((Q_ALL, HD), BF16),
            pltpu.VMEM((Q_ALL, HD), BF16),
            pltpu.VMEM((Q_ALL, HD), BF16),
            pltpu.VMEM((ROWS, 3 * TILE, Q_ALL), F32),
            pltpu.VMEM((ROWS, 3 * TILE, Q_ALL), F32),
            pltpu.VMEM((3 * TILE, Q_ALL), BF16),
            pltpu.VMEM((3 * TILE, Q_ALL), BF16),
            pltpu.VMEM((8, Q_ALL), F32),
            pltpu.VMEM((8, Q_ALL), F32),
            pltpu.VMEM((HD, Q_ALL), F32),
            pltpu.VMEM((HD, Q_ALL), F32),
            pltpu.VMEM((HD, Q_ALL), F32),
            pltpu.VMEM((HD, Q_ALL), F32),
            pltpu.VMEM((4, Q_ALL, HD), BF16),
            pltpu.SMEM((HEADS_HERE, 3), jnp.int32),
            dma((4,)),
            dma((2, 4)),
            dma((2, 4)),
            dma((2, 4)),
            dma((4, 5)),
            dma((7, 5)),
            dma((3, 5)),
            dma((9, 5)),
            dma((4, 4)),
            dma((3, 4)),
            dma,
        ],
        compiler_params=pltpu.CompilerParams(
            collective_id=0, has_side_effects=True, vmem_limit_bytes=48 * 1024 * 1024
        ),
    )(queries, keys, values, grad_out, head_window)


def solution(mesh):
    in_specs = (P("st", "hd"), P("st", "hd"), P("st", "hd"), P("st", "hd"), P("hd", None))
    out_specs = (P("st", "hd"), P("st", "hd"), P("st", "hd"), P("st", "hd"))
    return jax.shard_map(body, mesh=mesh, in_specs=in_specs, out_specs=out_specs, check_vma=False)
```

```python
import functools
import math

import jax
import jax.numpy as jnp
from jax import lax
from jax.experimental import pallas as pl
from jax.experimental.pallas import tpu as pltpu
from jax.sharding import PartitionSpec as P

HD = 128
TILE = 128
FRAMES = 4
HEADS_HERE = 3
SCALE = HD ** (-0.5)
EXP2_SCALE = SCALE * math.log2(math.e)
MESH = pl.DeviceIdType.MESH
BF16 = jnp.bfloat16
F32 = jnp.float32

OWN = ((0, 0), (0, 1), (1, 1), (1, 0))
HERE, OUT, IN = 0, 1, 2
ROWS = 9
K, V, Q, G, STATS = range(5)
Q_ALL = 4 * TILE


def blocks(lh):
    if lh < 2:
        return ((0, 0, 4 * TILE), (1, 0, 4 * TILE), (2, TILE, 2 * TILE))
    return ((0, 2 * TILE, 2 * TILE), (1, 2 * TILE, 2 * TILE), (2, 2 * TILE, TILE))


def pieces(lh):
    if lh < 2:
        return ((0, 2, 0, 4 * TILE), (2, 1, TILE, 2 * TILE))
    return ((0, 2, 2 * TILE, 2 * TILE), (2, 1, 2 * TILE, TILE))


def dot_nt(a, b):
    return lax.dot_general(a, b, (((1,), (1,)), ((), ())), preferred_element_type=F32)


def dot_tn(a, b):
    return lax.dot_general(a, b, (((0,), (0,)), ((), ())), preferred_element_type=F32)


def dot_nn(a, b):
    return lax.dot_general(a, b, (((1,), (0,)), ((), ())), preferred_element_type=F32)


def kernel(
    q_ref, k_ref, v_ref, g_ref, win_hbm,
    out_ref, gq_ref, gk_ref, gv_ref,
    kbuf, vbuf, qbuf, gbuf, stats, k_own, v_own, q_own, g_own, s_buf, dp_buf, p_low, ds_low, top_ref, sum_ref,
    out_t, gq_t, gk_t, gv_t, results, win_ref,
    own_send, own_recv, far_send, far_recv, chain_send, chain_recv, across_send, across_recv,
    fin_send, fin_recv, win_sem,
):
    pltpu.make_async_copy(win_hbm, win_ref, win_sem).start()
    inputs = (k_ref, v_ref, q_ref, g_ref)
    bufs = (kbuf, vbuf, qbuf, gbuf, stats)
    own = (k_own, v_own, q_own, g_own)
    place = lax.axis_index("st")
    t = place // 16
    upper = (place // 8) % 2
    col = (place // 2) % 4
    core = place % 2
    active = col < HEADS_HERE
    row = (place // 4) % 4
    column = place % 4
    w_half = column // 2
    lh_own = (row + upper) % 2
    lw_own = (column + w_half) % 2
    is_self = jnp.logical_and(active, w_half == core)
    outward = 2 * upper - 1
    t_out = t + outward
    t_in = t - outward
    has_out = jnp.logical_and(t_out >= 0, t_out < FRAMES)
    has_in = jnp.logical_and(t_in >= 0, t_in < FRAMES)
    other_core = place + 1 - 2 * core
    mate = place - 8 * outward
    outer = place + 8 * outward
    out2 = place + 16 * outward
    in2 = place - 16 * outward
    in3 = place - 24 * outward

    def worker(head):
        return (2 * t + upper) * 8 + 2 * head + w_half

    def owner(n):
        a, b = OWN[n]
        r = upper * (3 - a) + (1 - upper) * a
        c = core * (3 - b) + (1 - core) * b
        return t * 16 + r * 4 + c

    def far_owner(n, frame):
        a, b = OWN[n]
        r = upper * (3 - a) + (1 - upper) * a
        c = core * (3 - b) + (1 - core) * b
        return frame * 16 + r * 4 + c

    def remote(src, dst, send, recv, device):
        return pltpu.make_async_remote_copy(
            src_ref=src, dst_ref=dst, send_sem=send, recv_sem=recv,
            device_id={"st": device}, device_id_type=MESH,
        )

    def wait_for(dst, sem):
        pltpu.make_async_copy(dst, dst, sem).wait()

    barrier = pltpu.get_barrier_semaphore()

    def greet(device):
        pl.semaphore_signal(barrier, inc=1, device_id={"st": device}, device_id_type=MESH)

    at_edge = lh_own == 0

    def far_worker(side, head):
        return worker(head) + (-16, 16)[side] * outward

    far_flag = (has_in, has_out)
    for head in range(HEADS_HERE):
        @pl.when(worker(head) != place)
        def _():
            greet(worker(head))

        for side in range(2):
            @pl.when(jnp.logical_and(at_edge, far_flag[side]))
            def _():
                greet(far_worker(side, head))

    @pl.when(active)
    def _():
        for n in range(4):
            @pl.when(owner(n) != place)
            def _():
                greet(owner(n))

        greet(other_core)
        greet(mate)

        @pl.when(has_out)
        def _():
            greet(outer)
            greet(out2)
            for n in range(2):
                greet(far_owner(n, t_out))

        @pl.when(has_in)
        def _():
            greet(in2)
            greet(in3)
            for n in range(2):
                greet(far_owner(n, t_in))

    as_int = lambda flag: flag.astype(jnp.int32)
    selfs = as_int(is_self)
    greeted = 3 - selfs + 3 * as_int(at_edge) * (as_int(has_in) + as_int(has_out))
    pl.semaphore_wait(
        barrier, greeted + as_int(active) * (6 - selfs + 4 * as_int(has_out) + 4 * as_int(has_in))
    )

    def head_cols(ref, head):
        return ref.at[:, pl.ds(head * HD, HD)]

    def own_copy(which, head):
        return remote(
            head_cols(inputs[which], head), bufs[which].at[HERE, lh_own, lw_own],
            own_send.at[which], own_recv.at[lh_own, which], worker(head),
        )

    def far_copy(which, side, head):
        return remote(
            head_cols(inputs[which], head), bufs[which].at[(OUT, IN)[side], 0, lw_own],
            far_send.at[side, which], far_recv.at[side, which], far_worker(side, head),
        )

    def send_own(which):
        for head in range(HEADS_HERE):
            mine = worker(head) == place

            @pl.when(mine)
            def _():
                pltpu.make_async_copy(
                    head_cols(inputs[which], head), bufs[which].at[HERE, lh_own, lw_own], own_recv.at[lh_own, which]
                ).start()

            @pl.when(jnp.logical_not(mine))
            def _():
                own_copy(which, head).start()

    def own_left(which):
        ref = inputs[which]

        @pl.when(is_self)
        def _():
            wait_for(ref.at[:, pl.ds(0, (HEADS_HERE - 1) * HD)], own_send.at[which])

        @pl.when(jnp.logical_not(is_self))
        def _():
            wait_for(ref, own_send.at[which])

    def by_chain_at(head, half):
        if isinstance(head, int):
            low = jnp.logical_and(upper == 0, half == 0) if head == 2 else half < 0
            high = jnp.logical_and(upper == 1, half == head) if head < 2 else half < 0
            return jnp.logical_or(low, high)
        low = (upper == 0) & (half == 0) & (head == 2)
        return low | ((upper == 1) & (half == head) & (head < 2))

    by_chain = by_chain_at(col, core)
    skips = jnp.logical_or(upper == 1, w_half == 0)

    def send_far(which):
        for side in range(2):
            @pl.when(jnp.logical_and(at_edge, far_flag[side]))
            def _():
                for head in range(HEADS_HERE):
                    @pl.when(jnp.logical_not(by_chain_at(head, w_half)))
                    def _():
                        far_copy(which, side, head).start()

    for which in (K, Q, V, G):
        send_own(which)

    @pl.when(jnp.logical_not(active))
    def _():
        for which in (K, Q, V, G):
            own_left(which)
        for which in (K, V, Q, G):
            send_far(which)

    CHAIN = {
        1: ((HERE, 1), (HERE, 2), mate, None, None),
        2: ((HERE, 1), (OUT, 2), outer, has_out, has_out),
        3: ((HERE, 2), (OUT, 1), outer, has_out, has_out),
        4: ((HERE, 0), (OUT, 0), in2, has_in, has_out),
        5: ((HERE, 0), (IN, 0), out2, has_out, has_in),
        6: ((OUT, 2), (IN, 1), mate, has_out, has_in),
        7: ((OUT, 1), (IN, 2), mate, has_out, has_in),
    }
    STATS_TO = {
        1: CHAIN[1],
        2: CHAIN[2],
        3: ((HERE, 1), (OUT, 1), in2, has_in, has_out),
        4: CHAIN[4],
        5: CHAIN[5],
        6: ((HERE, 1), (IN, 1), out2, has_out, has_in),
        7: ((HERE, 1), (IN, 2), in3, has_in, has_in),
    }

    def route(which, number):
        return (STATS_TO if which == STATS else CHAIN)[number]

    def send_group(which, number):
        sent = route(which, number)[3]
        if number == 5 and which != STATS:
            return 3
        return 0 if sent is None else 1 if sent is has_out else 2

    def routes_of(which):
        return (1, 2, 3, 6, 7) if which != STATS else (1, 2, 3, 4, 5, 6, 7)

    def only(flag, run):
        if flag is None:
            run()
        else:
            pl.when(flag)(run)

    def chain_copy(which, number):
        buf = bufs[which]
        (f0, a0), (f1, a1), device, _, _ = route(which, number)
        return remote(
            buf.at[f0, a0, pl.ds(0, 2)], buf.at[f1, a1, pl.ds(0, 2)],
            chain_send.at[send_group(which, number), which], chain_recv.at[number - 1, which], device,
        )

    def across_copy(which, f, a):
        buf = bufs[which]
        return remote(
            buf.at[f, a, 1], buf.at[f, a, 2], across_send.at[f, which], across_recv.at[f * 3 + a, which], other_core
        )

    def fin_parts(which, n):
        dst = (out_ref, gq_ref, gk_ref, gv_ref)[which]
        return (
            results.at[which, pl.ds(n * TILE, TILE), :],
            dst.at[:, pl.ds(pl.multiple_of(col * HD, HD), HD)],
        )

    def fin_copy(which, n):
        src, dst = fin_parts(which, n)
        return remote(src, dst, fin_send.at[n, which], fin_recv.at[col, which], owner(n))

    def send_fin(which):
        for n in range(4):
            mine = owner(n) == place

            @pl.when(mine)
            def _():
                src, dst = fin_parts(which, n)
                pltpu.make_async_copy(src, dst, fin_recv.at[col, which]).start()

            @pl.when(jnp.logical_not(mine))
            def _():
                fin_copy(which, n).start()

    def exists(f):
        return (None, has_out, has_in)[f]

    pltpu.make_async_copy(win_hbm, win_ref, win_sem).wait()

    @pl.when(active)
    def _():
        at_head = jnp.minimum(col, HEADS_HERE - 1)
        win_t = win_ref[at_head, 0]
        win_h = win_ref[at_head, 1]
        win_w = win_ref[at_head, 2]

        def bias(f, a, b, first, count):
            q_tile = lax.broadcasted_iota(jnp.int32, (1, count), 1) // TILE + first // TILE
            q_lh = q_tile // 2
            q_lw = ((q_tile + 1) // 2) % 2
            bad = jnp.maximum(jnp.abs(q_lh - a) - win_h, jnp.abs(q_lw - b) - win_w)
            if f != HERE:
                bad = jnp.maximum(bad, 1 - win_t)
            return jnp.where(bad > 0, -jnp.inf, 0.0).astype(F32)

        def score_row(f, a):
            def run():
                for b, first, count in blocks(a):
                    lanes = slice(first, first + count)
                    s = dot_nt(kbuf[f, a, b], q_own[lanes, :]) + bias(f, a, b, first, count)
                    s_buf[f * 3 + a, b * TILE : (b + 1) * TILE, lanes] = s
                    top_ref[:, lanes] = jnp.maximum(
                        top_ref[:, lanes], jnp.max(s.reshape(TILE // 8, 8, count), axis=0)
                    )

            only(exists(f), run)

        def exp_row(f, a):
            def run():
                for b, first, count in blocks(a):
                    lanes = slice(first, first + count)
                    keys = slice(b * TILE, (b + 1) * TILE)
                    e = jnp.exp2((s_buf[f * 3 + a, keys, lanes] - top_ref[:1, lanes]) * EXP2_SCALE)
                    s_buf[f * 3 + a, keys, lanes] = e
                    sum_ref[:, lanes] += jnp.sum(e.reshape(TILE // 8, 8, count), axis=0)

            only(exists(f), run)

        def v_row(f, a):
            def run():
                for b, first, count in blocks(a):
                    lanes = slice(first, first + count)
                    keys = slice(b * TILE, (b + 1) * TILE)
                    p = s_buf[f * 3 + a, keys, lanes] * sum_ref[:1, lanes]
                    s_buf[f * 3 + a, keys, lanes] = p
                    p_low[keys, lanes] = p.astype(BF16)
                    dp_buf[f * 3 + a, keys, lanes] = dot_nt(vbuf[f, a, b], g_own[lanes, :])
                for b, n, first, count in pieces(a):
                    lanes = slice(first, first + count)
                    keys = slice(b * TILE, (b + n) * TILE)
                    vals = vbuf[f, a, b : b + n].reshape(n * TILE, HD)
                    out_t[:, lanes] += dot_tn(vals, p_low[keys, lanes])

            only(exists(f), run)

        def dq_row(f, a):
            def run():
                for b, first, count in blocks(a):
                    lanes = slice(first, first + count)
                    keys = slice(b * TILE, (b + 1) * TILE)
                    ds = s_buf[f * 3 + a, keys, lanes] * (dp_buf[f * 3 + a, keys, lanes] - top_ref[:1, lanes])
                    ds_low[keys, lanes] = ds.astype(BF16)
                for b, n, first, count in pieces(a):
                    lanes = slice(first, first + count)
                    keys = slice(b * TILE, (b + n) * TILE)
                    vals = kbuf[f, a, b : b + n].reshape(n * TILE, HD)
                    gq_t[:, lanes] += dot_tn(vals, ds_low[keys, lanes])

            only(exists(f), run)

        def kv_row(f, a):
            def run():
                for b, first, count in blocks(a):
                    lanes = slice(first, first + count)
                    rows = slice(b * TILE, (b + 1) * TILE)
                    of_query = stats[f, a, b].T
                    top, inverse, delta = of_query[:, 0:1], of_query[:, 1:2], of_query[:, 2:3]
                    s = dot_nt(qbuf[f, a, b], k_own[lanes, :]) + bias(f, a, b, first, count)
                    p = jnp.exp2((s - top) * EXP2_SCALE) * inverse
                    p_low[rows, lanes] = p.astype(BF16)
                    dp = dot_nt(gbuf[f, a, b], v_own[lanes, :])
                    ds_low[rows, lanes] = (p * (dp - delta)).astype(BF16)
                for b, n, first, count in pieces(a):
                    lanes = slice(first, first + count)
                    rows = slice(b * TILE, (b + n) * TILE)
                    gv_t[:, lanes] += dot_tn(gbuf[f, a, b : b + n].reshape(n * TILE, HD), p_low[rows, lanes])
                    gk_t[:, lanes] += dot_tn(qbuf[f, a, b : b + n].reshape(n * TILE, HD), ds_low[rows, lanes])

            only(exists(f), run)

        def chain_go(which, *numbers):
            for number in numbers:
                only(route(which, number)[3], lambda: chain_copy(which, number).start())

        def chain_arrive(which, number):
            def run():
                chain_copy(which, number).wait_recv()
                across_copy(which, *route(which, number)[1]).start()

            only(route(which, number)[4], run)

        def across_arrive(which, f, a):
            only(exists(f), lambda: across_copy(which, f, a).wait_recv())

        def own_arrive(which, a):
            wait_for(bufs[which].at[HERE, a, pl.ds(0, 2)], own_recv.at[a, which])
            across_copy(which, HERE, a).start()

        def keep_own(which):
            for n in range(4):
                own[which][n * TILE : (n + 1) * TILE, :] = bufs[which][HERE, OWN[n][0], OWN[n][1]]

        def gather_first(which):
            own_arrive(which, 1)
            chain_go(which, 1, 2)
            own_arrive(which, 0)

        def gather_second(which):
            chain_arrive(which, 1)
            chain_go(which, 3)
            chain_arrive(which, 2)
            chain_go(which, 6)

        def gather_third(which):
            chain_arrive(which, 3)
            chain_go(which, 7)

        def gather_rest(which):
            def far_arrive(side):
                f = (OUT, IN)[side]

                @pl.when(by_chain)
                def _():
                    chain_copy(which, 4 + side).wait_recv()

                @pl.when(jnp.logical_not(by_chain))
                def _():
                    wait_for(bufs[which].at[f, 0, pl.ds(0, 2)], far_recv.at[side, which])

                across_copy(which, f, 0).start()

            pl.when(has_out)(lambda: far_arrive(0))
            pl.when(has_in)(lambda: far_arrive(1))
            for number in (6, 7):
                chain_arrive(which, number)

        def all_lanes(value):
            return jnp.broadcast_to(value, (8, Q_ALL))

        def go_far(which):
            send_far(which)

            @pl.when(by_chain)
            def _():
                chain_go(which, 4, 5)

        gather_first(K)
        own_arrive(Q, 1)
        own_arrive(Q, 0)
        keep_own(Q)
        for which in (K, Q, V):
            own_left(which)
        go_far(K)
        gather_first(V)
        go_far(V)
        top_ref[...] = jnp.full((8, Q_ALL), -jnp.inf, F32)
        for a in (0, 1):
            across_arrive(K, HERE, a)
            score_row(HERE, a)
        gather_second(K)
        gather_second(V)
        chain_go(Q, 1, 2)
        across_arrive(K, HERE, 2)
        score_row(HERE, 2)
        across_arrive(K, OUT, 2)
        score_row(OUT, 2)
        gather_third(K)
        gather_third(V)
        gather_first(G)
        own_left(G)
        across_arrive(K, OUT, 1)
        score_row(OUT, 1)
        gather_rest(K)
        gather_second(Q)
        go_far(Q)
        across_arrive(K, OUT, 0)
        score_row(OUT, 0)
        for a in range(3):
            across_arrive(K, IN, a)
            score_row(IN, a)
        gather_second(G)
        go_far(G)
        for which in (K, V, G):
            keep_own(which)
        top_ref[...] = all_lanes(jnp.max(top_ref[...], axis=0, keepdims=True))
        stats[HERE, :2, :2] = jnp.zeros((2, 2, 8, TILE), F32)
        for n, (a, b) in enumerate(OWN):
            stats[HERE, a, b, 0:1, :] = top_ref[:1, n * TILE : (n + 1) * TILE]
        sum_ref[...] = jnp.zeros((8, Q_ALL), F32)
        for ref in (out_t, gq_t, gk_t, gv_t):
            ref[...] = jnp.zeros((HD, Q_ALL), F32)
        for f in range(3):
            for a in range(3):
                exp_row(f, a)
        sum_ref[...] = all_lanes(1.0 / jnp.sum(sum_ref[...], axis=0, keepdims=True))
        for n, (a, b) in enumerate(OWN):
            stats[HERE, a, b, 1:2, :] = sum_ref[:1, n * TILE : (n + 1) * TILE]
        gather_third(Q)
        for f, a in ((HERE, 0), (HERE, 1), (HERE, 2), (OUT, 2), (OUT, 1)):
            across_arrive(V, f, a)
            v_row(f, a)
        gather_third(G)
        gather_rest(V)
        for f, a in ((OUT, 0), (IN, 0), (IN, 1), (IN, 2)):
            across_arrive(V, f, a)
            v_row(f, a)
        for n, (a, b) in enumerate(OWN):
            lanes = slice(n * TILE, (n + 1) * TILE)
            o_t = out_t[:, lanes]
            g_t = g_own[lanes, :].astype(F32).T
            delta = jnp.sum(o_t * g_t, axis=0, keepdims=True)
            top_ref[:, lanes] = jnp.broadcast_to(delta, (8, TILE))
            stats[HERE, a, b, 2:3, :] = delta
        chain_go(STATS, 7, 3, 6, 4, 5, 2, 1)
        across_copy(STATS, HERE, 1).start()
        across_copy(STATS, HERE, 0).start()

        def give(which, total, factor):
            for n in range(4):
                lanes = slice(n * TILE, (n + 1) * TILE)
                results[which, lanes, :] = (total[:, lanes] * factor).T.astype(BF16)
            send_fin(which)

        give(0, out_t, 1.0)
        for a in range(3):
            dq_row(HERE, a)
        for a in range(2):
            for which in (Q, G, STATS):
                across_arrive(which, HERE, a)
            kv_row(HERE, a)
        gather_rest(Q)
        for a in range(3):
            dq_row(OUT, a)
        gather_rest(G)
        for a in range(3):
            dq_row(IN, a)
        give(1, gq_t, SCALE)
        for arrivals, rows in (
            ((1, 2, 3), ((HERE, 2),)),
            ((4, 5), ((OUT, 2), (OUT, 1))),
            ((6, 7), ((OUT, 0), (IN, 0), (IN, 1), (IN, 2))),
        ):
            for number in arrivals:
                chain_arrive(STATS, number)
            for f, a in rows:
                for which in (Q, G, STATS):
                    across_arrive(which, f, a)
                kv_row(f, a)
        give(2, gk_t, SCALE)
        give(3, gv_t, 1.0)

    for head in range(HEADS_HERE):
        for which, ref in enumerate((out_ref, gq_ref, gk_ref, gv_ref)):
            wait_for(ref.at[:, pl.ds(head * HD, HD)], fin_recv.at[head, which])

    for which in range(4):
        for side in range(2):
            sends = jnp.logical_and(at_edge, far_flag[side])

            @pl.when(jnp.logical_and(sends, skips))
            def _():
                wait_for(inputs[which].at[:, pl.ds(0, (HEADS_HERE - 1) * HD)], far_send.at[side, which])

            @pl.when(jnp.logical_and(sends, jnp.logical_not(skips)))
            def _():
                wait_for(inputs[which], far_send.at[side, which])

    @pl.when(active)
    def _():
        for which in range(5):
            buf = bufs[which]
            for group in range(4):
                numbers = [x for x in routes_of(which) if send_group(which, x) == group]
                if numbers:
                    if len(numbers) == 4:
                        rows = buf.at[pl.ds(0, 2), pl.ds(0, 2), pl.ds(0, 2)]
                    else:
                        rows = buf.at[HERE, pl.ds(0, len(numbers)), pl.ds(0, 2)]
                    only(route(which, numbers[0])[3], lambda: wait_for(rows, chain_send.at[group, which]))
            if which != STATS:
                for number in (4, 5):
                    @pl.when(jnp.logical_and(by_chain, CHAIN[number][3]))
                    def _():
                        chain_copy(which, number).wait_send()

            for f in range(3):
                only(exists(f), lambda: wait_for(buf.at[f, 0], across_send.at[f, which]))
        for n in range(4):
            @pl.when(owner(n) != place)
            def _():
                for which in range(4):
                    fin_copy(which, n).wait_send()


def body(queries, keys, values, grad_out, head_window):
    shape = jax.ShapeDtypeStruct((TILE, HEADS_HERE * HD), BF16)
    hbm = pl.BlockSpec(memory_space=pltpu.HBM)
    dma = pltpu.SemaphoreType.DMA
    return pl.pallas_call(
        kernel,
        out_shape=(shape,) * 4,
        in_specs=[hbm] * 5,
        out_specs=(hbm,) * 4,
        scratch_shapes=[
            pltpu.VMEM((3, 3, 3, TILE, HD), BF16),
            pltpu.VMEM((3, 3, 3, TILE, HD), BF16),
            pltpu.VMEM((3, 3, 3, TILE, HD), BF16),
            pltpu.VMEM((3, 3, 3, TILE, HD), BF16),
            pltpu.VMEM((3, 3, 3, 8, TILE), F32),
            pltpu.VMEM((Q_ALL, HD), BF16),
            pltpu.VMEM((Q_ALL, HD), BF16),
            pltpu.VMEM((Q_ALL, HD), BF16),
            pltpu.VMEM((Q_ALL, HD), BF16),
            pltpu.VMEM((ROWS, 3 * TILE, Q_ALL), F32),
            pltpu.VMEM((ROWS, 3 * TILE, Q_ALL), F32),
            pltpu.VMEM((3 * TILE, Q_ALL), BF16),
            pltpu.VMEM((3 * TILE, Q_ALL), BF16),
            pltpu.VMEM((8, Q_ALL), F32),
            pltpu.VMEM((8, Q_ALL), F32),
            pltpu.VMEM((HD, Q_ALL), F32),
            pltpu.VMEM((HD, Q_ALL), F32),
            pltpu.VMEM((HD, Q_ALL), F32),
            pltpu.VMEM((HD, Q_ALL), F32),
            pltpu.VMEM((4, Q_ALL, HD), BF16),
            pltpu.SMEM((HEADS_HERE, 3), jnp.int32),
            dma((4,)),
            dma((2, 4)),
            dma((2, 4)),
            dma((2, 4)),
            dma((4, 5)),
            dma((7, 5)),
            dma((3, 5)),
            dma((9, 5)),
            dma((4, 4)),
            dma((3, 4)),
            dma,
        ],
        compiler_params=pltpu.CompilerParams(
            collective_id=0, has_side_effects=True, vmem_limit_bytes=48 * 1024 * 1024
        ),
    )(queries, keys, values, grad_out, head_window)


def solution(mesh):
    in_specs = (P("st", "hd"), P("st", "hd"), P("st", "hd"), P("st", "hd"), P("hd", None))
    out_specs = (P("st", "hd"), P("st", "hd"), P("st", "hd"), P("st", "hd"))
    return jax.shard_map(body, mesh=mesh, in_specs=in_specs, out_specs=out_specs, check_vma=False)
```
